32 devices in a mesh: seq: 8 (over z, core), tensor: 4 (over y, x).
Axes of the slice: x: 2, y: 2, z: 4, core: 2. Of those that a mesh axis runs over, the one named last changes fastest.
Arguments:
- qkv: bfloat16 [3, 2048, 8192], P(None, 'seq', 'tensor'), may hold values from -6 to 6
- conv_weight: float32 [3, 3, 8192], P(None, None, 'tensor'), may hold values from -3.6 to 3.6
- decay_rate: float32 [16, 8192], P(None, 'tensor'), may hold values from 1e-05 to 0.06
- residue: float32 [16, 8192], P(None, 'tensor'), may hold values from -3 to 3
- skip_gain: float32 [8192], P('tensor'), may hold values from -5 to 5
- out_weight: bfloat16 [8192, 8192], P('seq', 'tensor'), may hold values from -0.09375 to 0.09375
Outputs:
- mixer_out: bfloat16 [2048, 8192], P('seq', 'tensor')
The draws below stay inside these ranges and needn't reach their ends.
All inputs are finite; a program needn't handle non-finite values.
Results may differ from the reference program's by a relative error of at most 0.0049.
Values may be sent and summed in bfloat16 or wider, within the bound.
A program may use at most 128 MiB of HBM per device.

```python
import math
from functools import partial
import jax
import jax.numpy as jnp
from jax import lax

D = 8192
M = 16
KS = 3
TOK_DEV = 256
TOKENS = 2048


def draw_decay_rate(key, part):
    key_pick, key_slow, key_fast = jax.random.split(key, 3)
    share_slow = 0.5
    slow_top = 1.0 / TOKENS
    picked = jax.random.uniform(key_pick, (M, D), jnp.float32) < share_slow
    slow_values = jnp.exp(math.log(1e-05) + jax.random.uniform(key_slow, (M, D), jnp.float32) * (math.log(slow_top) - math.log(1e-05)))
    fast_values = jnp.exp(math.log(slow_top) + jax.random.uniform(key_fast, (M, D), jnp.float32) * (math.log(0.06) - math.log(slow_top)))
    return jnp.clip(jnp.where(picked, slow_values, fast_values), 1e-05, 0.06).astype(jnp.float32)


def raised(drawn, stream_key, source, target, parts, factor):
    def block_of(dim):
        return (jnp.arange(drawn.shape[dim]) // (drawn.shape[dim] // parts)).reshape((-1,) + (1,) * (drawn.ndim - 1 - dim))

    first = jax.random.permutation(stream_key, parts)[block_of(target)]
    second = (block_of(target) + parts // 2) % parts
    return jnp.where((block_of(source) == first) | (block_of(source) == second), factor * drawn, drawn)


def level_of(rng, dims, shards, low, top_value):
    gain, own = 1.0, jax.random.fold_in(rng, 6)
    for dim, shards_of in shards:
        heights = jnp.exp(jax.random.uniform(jax.random.fold_in(own, dim), (shards_of,), jnp.float32, low / len(shards), top_value / len(shards)))
        gain = gain * jnp.repeat(heights, dims[dim] // shards_of).reshape([-1 if axis == dim else 1 for axis in range(len(dims))])
    return gain


def normal_values(own_key, dims, scale, bound, cuts=(), kind=jnp.bfloat16):
    array = scale * jax.random.normal(own_key, dims, jnp.float32)
    if cuts:
        array = array * level_of(own_key, dims, cuts, -0.22, 0.18)
    return jnp.clip(array, -bound, bound).astype(kind)


def gaussian_with(own_key, extent, spread, bound, shards, heavy, kind=jnp.bfloat16):
    values = spread * jax.random.normal(own_key, extent, jnp.float32)
    if shards:
        values = values * level_of(own_key, extent, shards, -0.22, 0.18)
    return jnp.clip(raised(values, jax.random.fold_in(own_key, 3), *heavy), -bound, bound).astype(kind)


def setup_inputs(seed: int = 0) -> dict:
    splits = jax.random.split(jax.random.key(seed), 7)
    return {
        "qkv": normal_values(splits[0], (3, TOKENS, D), 1.0, 6.0, ((1, 8), (2, 4))),
        "conv_weight": normal_values(splits[1], (3, KS, D), 0.6, 3.6, ((2, 4),), jnp.float32),
        "decay_rate": draw_decay_rate(jax.random.fold_in(splits[6], 71), 0),
        "residue": normal_values(splits[3], (M, D), 0.5, 3.0, ((1, 4),), jnp.float32),
        "skip_gain": normal_values(splits[4], (D,), 1.0, 5.0, ((0, 4),), jnp.float32),
        "out_weight": gaussian_with(splits[5], (D, D), D ** -0.5, 0.09375, ((0, 8), (1, 4)), (0, 1, 8, 2.0)),
    }


PRECISE = lax.Precision.HIGHEST

def short_filter(padded, conv_weight, length):
    result = jnp.zeros((padded.shape[0], length, padded.shape[2]), jnp.float32)
    for offset in range(KS):
        start_row = KS - 1 - offset
        result = result + conv_weight[:, offset, None, :] * padded[:, start_row:start_row + length, :]
    return result

def mode_tables(rate_block, residue_block, length):
    lag_values = jnp.arange(length, dtype=jnp.float32)
    decay_table = jnp.exp(-rate_block[:, None, :] * lag_values[None, :, None])
    mode_weight = residue_block * jnp.sqrt(-jnp.expm1(-2.0 * rate_block))
    return (decay_table, mode_weight)

def toeplitz(filter_taps):
    length = filter_taps.shape[0]
    lag_index = jnp.arange(length)[:, None] - jnp.arange(length)[None, :]
    picked = filter_taps[jnp.maximum(lag_index, 0), :]
    return jnp.where(lag_index[:, :, None] >= 0, picked, 0.0)

def modal_block(block_len, inputs):
    x_block, rate_block, residue_block = inputs
    decay_table, mode_weight = mode_tables(rate_block, residue_block, block_len)
    filter_taps = jnp.einsum('mc,mdc->dc', mode_weight, decay_table, precision=PRECISE)
    matrix = toeplitz(filter_taps)
    inner_part = jnp.einsum('tsc,nsc->ntc', matrix, x_block, precision=PRECISE)
    local_state = jnp.einsum('msc,nsc->nmc', decay_table[:, ::-1, :], x_block, precision=PRECISE)
    block_decay = jnp.exp(-rate_block * block_len)

    def advance(state, segment):
        return (state * block_decay + segment, state)
    _, entering = lax.scan(advance, jnp.zeros(rate_block.shape, jnp.float32), local_state)
    later_table = decay_table * jnp.exp(-rate_block)[:, None, :]
    carried = jnp.einsum('mc,mdc,nmc->ndc', mode_weight, later_table, entering, precision=PRECISE)
    return inner_part + carried

def reference(qkv, conv_weight, decay_rate, residue, skip_gain, out_weight):
    length = qkv.shape[1]
    features_in = qkv.astype(jnp.float32)
    padded = jnp.pad(features_in, ((0, 0), (KS - 1, 0), (0, 0)))
    filtered = short_filter(padded, conv_weight, length)
    product = filtered[1] * filtered[2]
    channels = product.shape[1]
    group_width = min(channels, 128)
    groups = channels // group_width
    block_len = min(TOK_DEV, 64)
    block_count = length // block_len
    x_groups = product.reshape(block_count, block_len, groups, group_width).transpose(2, 0, 1, 3)
    rate_groups = decay_rate.reshape(M, groups, group_width).transpose(1, 0, 2)
    residue_groups = residue.reshape(M, groups, group_width).transpose(1, 0, 2)
    long_groups = lax.map(partial(modal_block, block_len), (x_groups, rate_groups, residue_groups))
    long_part = long_groups.transpose(1, 2, 0, 3).reshape(length, channels)
    long_part = long_part + skip_gain[None, :] * product
    mixed = (filtered[0] * long_part).astype(jnp.bfloat16)
    return jnp.dot(mixed, out_weight, preferred_element_type=jnp.float32).astype(jnp.bfloat16)
```

```python
import functools

import jax
import jax.numpy as jnp
from jax import lax
from jax.experimental import pallas as pl
from jax.experimental.pallas import tpu as pltpu
from jax.sharding import PartitionSpec as P

MESH = pl.DeviceIdType.MESH
LANES = 128
HALO = 16


def kernel(
    ns,
    nt,
    modes,
    qkv,
    conv_w,
    decay,
    decay_sec,
    gain,
    skip,
    weight,
    out,
    halo,
    ext,
    prod,
    qf,
    mixed,
    wfull,
    state,
    other,
    total,
    totals,
    enter,
    stage,
    full,
    part,
    recv,
    own,
    halo_sem,
    w_sem,
    swap_sem,
    tot_send,
    tot_recv,
    s1_send,
    s1_recv,
    s2_send,
    s2_recv,
    s3_send,
    s3_recv,
    rs_send,
    rs_recv,
    loc_sem,
):
    nz = ns // 2
    tok = qkv.shape[1]
    ch = qkv.shape[2]
    groups = ch // LANES
    quarter = tok // nt
    rows_w = weight.shape[0]
    cols = weight.shape[1]
    s = lax.axis_index("seq")
    t = lax.axis_index("tensor")
    z = s // 2
    c = s % 2
    mate = 2 * z + (1 - c)

    def dev(seq, ten):
        return (seq, ten)

    barrier = pltpu.get_barrier_semaphore()
    for d in range(1, ns):
        pl.semaphore_signal(barrier, inc=1, device_id=dev((s + d) % ns, t), device_id_type=MESH)
    for d in range(1, nt):
        pl.semaphore_signal(barrier, inc=1, device_id=dev(s, (t + d) % nt), device_id_type=MESH)
    pl.semaphore_wait(barrier, ns - 1 + nt - 1)

    halo_copy = pltpu.make_async_remote_copy(
        src_ref=qkv.at[:, pl.ds(tok - HALO, HALO), :],
        dst_ref=halo,
        send_sem=halo_sem.at[0],
        recv_sem=halo_sem.at[1],
        device_id=dev((s + 1) % ns, t),
        device_id_type=MESH,
    )

    @pl.when(s < ns - 1)
    def _():
        halo_copy.start()

    w_rows = pl.ds(pl.multiple_of(c * rows_w, rows_w), rows_w)
    w_remote = pltpu.make_async_remote_copy(
        src_ref=weight,
        dst_ref=wfull.at[w_rows, :],
        send_sem=w_sem.at[0],
        recv_sem=w_sem.at[1],
        device_id=dev(mate, t),
        device_id_type=MESH,
    )
    w_remote.start()
    w_local = pltpu.make_async_copy(weight, wfull.at[w_rows, :], w_sem.at[2])
    w_local.start()

    @pl.when(s == 0)
    def _():
        halo[...] = jnp.zeros_like(halo)

    @pl.when(s > 0)
    def _():
        halo_copy.wait_recv()

    def short(i, lanes):
        ext[i, 0:HALO, :] = halo[i, :, lanes].astype(jnp.float32)
        ext[i, HALO : HALO + tok, :] = qkv[i, :, lanes].astype(jnp.float32)
        taps = conv_w[pl.ds(3 * i, 3), lanes]
        return (
            taps[0:1] * ext[i, HALO : HALO + tok, :]
            + taps[1:2] * ext[i, HALO - 1 : HALO - 1 + tok, :]
            + taps[2:3] * ext[i, HALO - 2 : HALO - 2 + tok, :]
        )

    for g in range(groups):
        lanes = pl.ds(g * LANES, LANES)
        prod[pl.ds(g, tok, stride=groups), :] = short(1, lanes) * short(2, lanes)

    width = min(8, groups)

    def mode_rows(ref, m, h):
        return ref[m * groups + h * width : m * groups + (h + 1) * width, :]

    def tree(values):
        while len(values) > 1:
            values = [a + b for a, b in zip(values[::2], values[1::2])] + (
                [values[-1]] if len(values) % 2 else []
            )
        return values[0]

    for h in range(groups // width):
        skips = skip[h * width : (h + 1) * width, :]

        def step(i, states, h=h, skips=skips):
            rows = pl.ds(pl.multiple_of(i * groups + h * width, width), width)
            x = prod[rows, :]
            new = tuple(st * mode_rows(decay, m, h) + x for m, st in enumerate(states))
            terms = [st * mode_rows(gain, m, h) for m, st in enumerate(new)]
            prod[rows, :] = tree(terms) + skips * x
            return new

        states = lax.fori_loop(
            0,
            tok,
            step,
            tuple(jnp.zeros((width, LANES), jnp.float32) for _ in range(modes)),
            unroll=4,
        )
        for m in range(modes):
            state[m * groups + h * width : m * groups + (h + 1) * width, :] = states[m]

    swap = pltpu.make_async_remote_copy(
        src_ref=state,
        dst_ref=other,
        send_sem=swap_sem.at[0],
        recv_sem=swap_sem.at[1],
        device_id=dev(mate, t),
        device_id_type=MESH,
    )
    swap.start()
    swap.wait_recv()

    @pl.when(c == 0)
    def _():
        total[...] = (decay_sec[...] * state[...] + other[...]).astype(total.dtype)

    @pl.when(c == 1)
    def _():
        total[...] = (decay_sec[...] * other[...] + state[...]).astype(total.dtype)

    def tot_copy(target, source):
        return pltpu.make_async_remote_copy(
            src_ref=total,
            dst_ref=totals.at[source],
            send_sem=tot_send.at[target],
            recv_sem=tot_recv.at[source],
            device_id=dev(2 * target + c, t),
            device_id_type=MESH,
        )

    for k in range(1, nz):

        @pl.when(k > z)
        def _(k=k):
            tot_copy(k, z).start()

    for g in range(groups):
        lanes = pl.ds(g * LANES, LANES)
        qf[:, lanes] = short(0, lanes)

    enter[...] = jnp.zeros_like(enter)
    for k in range(nz - 1):

        @pl.when(k < z)
        def _(k=k):
            tot_copy(z, k).wait_recv()
            enter[...] = enter[...] * decay_sec[...] * decay_sec[...] + totals[k].astype(
                jnp.float32
            )

    @pl.when(c == 1)
    def _():
        enter[...] = decay_sec[...] * enter[...] + other[...]

    for h in range(groups // width):

        def fix(i, carried, h=h):
            rows = pl.ds(pl.multiple_of(i * groups + h * width, width), width)
            prod[rows, :] = prod[rows, :] + tree(list(carried))
            return tuple(u * mode_rows(decay, m, h) for m, u in enumerate(carried))

        lax.fori_loop(
            0,
            tok,
            fix,
            tuple(
                mode_rows(gain, m, h) * mode_rows(decay, m, h) * mode_rows(enter, m, h)
                for m in range(modes)
            ),
            unroll=4,
        )

    for g in range(groups):
        lanes = pl.ds(g * LANES, LANES)
        mixed[:, lanes] = (qf[:, lanes] * prod[pl.ds(g, tok, stride=groups), :]).astype(
            mixed.dtype
        )

    def share(index):
        return pl.ds(pl.multiple_of(index * quarter, quarter), quarter)

    def s1_copy(target, source):
        return pltpu.make_async_remote_copy(
            src_ref=mixed.at[share(target), :],
            dst_ref=stage.at[source],
            send_sem=s1_send.at[target],
            recv_sem=s1_recv.at[source],
            device_id=dev(s, target),
            device_id_type=MESH,
        )

    def each_peer(body):
        def one(d, carry):
            body((t + d) % nt)
            return carry

        lax.fori_loop(1, nt, one, 0)

    each_peer(lambda q: s1_copy(q, t).start())
    own_copy = pltpu.make_async_copy(mixed.at[share(t), :], stage.at[t], loc_sem.at[0])
    own_copy.start()
    own_copy.wait()
    each_peer(lambda q: s1_copy(t, q).wait_recv())

    def s2_copy(target, source):
        return pltpu.make_async_remote_copy(
            src_ref=stage.at[target],
            dst_ref=full.at[source, share(t), :],
            send_sem=s2_send.at[target],
            recv_sem=s2_recv.at[source],
            device_id=dev(2 * target + c, t),
            device_id_type=MESH,
        )

    candidates = 2 * (nz - 1)

    def each_plane(e, body):
        d = nz - 1 - e // 2
        k = z + d * (1 - 2 * (e % 2))

        @pl.when((k >= 0) & (k < nz))
        def _():
            body(k)

    def loop_planes(body):
        def one(e, carry):
            each_plane(e, body)
            return carry

        lax.fori_loop(0, candidates, one, 0)

    loop_planes(lambda k: s2_copy(k, z).start())
    keep = pltpu.make_async_copy(stage.at[z], full.at[z, share(t), :], loc_sem.at[1])
    keep.start()
    keep.wait()

    def s3_copy(target, source, k):
        rows = full.at[k, share(source), :]
        return pltpu.make_async_remote_copy(
            src_ref=rows,
            dst_ref=rows,
            send_sem=s3_send.at[k, target],
            recv_sem=s3_recv.at[k, source],
            device_id=dev(s, target),
            device_id_type=MESH,
        )

    def spread(k):
        each_peer(lambda q: s3_copy(q, t, k).start())

    def spread_received(k):
        s2_copy(z, k).wait_recv()
        spread(k)

    def gathered(k):
        each_peer(lambda q: s3_copy(t, q, k).wait_recv())

    tile = min(512, cols)

    def product(k, store):
        def one(n, carry):
            lanes = pl.ds(pl.multiple_of(n * tile, tile), tile)
            store(
                lanes,
                jnp.dot(full[k], wfull[:, lanes], preferred_element_type=jnp.float32),
            )
            return carry

        lax.fori_loop(0, cols // tile, one, 0)

    def rs_copy(k, slot, target, source_slot):
        return pltpu.make_async_remote_copy(
            src_ref=part.at[k],
            dst_ref=recv.at[slot],
            send_sem=rs_send.at[k],
            recv_sem=rs_recv.at[slot],
            device_id=dev(2 * target + c, t),
            device_id_type=MESH,
        )

    def rs_wait(slot):
        rs_copy(z, slot, z, slot).wait_recv()

    def contribute(k):
        gathered(k)

        def fresh(lanes, value):
            part[k, :, lanes] = value.astype(part.dtype)

        def added(lanes, value):
            part[k, :, lanes] = (value + recv[k, :, lanes].astype(jnp.float32)).astype(part.dtype)

        @pl.when((k > z) & (z > 0))
        def _():
            rs_wait(k)
            product(k, added)

        @pl.when((k < z) & (z < nz - 1))
        def _():
            rs_wait(k)
            product(k, added)

        @pl.when(((k > z) & (z == 0)) | ((k < z) & (z == nz - 1)))
        def _():
            product(k, fresh)

        @pl.when(k > z)
        def _():
            rs_copy(k, k, z + 1, k).start()

        @pl.when((k < z) & (k < z - 1))
        def _():
            rs_copy(k, k, z - 1, k).start()

        @pl.when((k < z) & (k == z - 1))
        def _():
            rs_copy(k, nz, z - 1, k).start()

    spread(z)
    w_local.wait()
    w_remote.wait_recv()

    lead = 2
    for e in range(lead):
        each_plane(e, spread_received)
    gathered(z)

    def keep_own(lanes, value):
        own[:, lanes] = value

    product(z, keep_own)

    def one_plane(e, carry):
        @pl.when(e + lead < candidates)
        def _():
            each_plane(e + lead, spread_received)

        each_plane(e, contribute)
        return carry

    lax.fori_loop(0, candidates, one_plane, 0)

    @pl.when(z > 0)
    def _():
        rs_wait(z)
        own[...] += recv[z].astype(jnp.float32)

    @pl.when(z < nz - 1)
    def _():
        rs_wait(nz)
        own[...] += recv[nz].astype(jnp.float32)

    out[...] = own[...].astype(out.dtype)

    @pl.when(s < ns - 1)
    def _():
        halo_copy.wait_send()

    w_remote.wait_send()
    swap.wait_send()
    for k in range(1, nz):

        @pl.when(k > z)
        def _(k=k):
            tot_copy(k, z).wait_send()

    each_peer(lambda q: s1_copy(q, t).wait_send())
    loop_planes(lambda k: s2_copy(k, z).wait_send())

    def all_sent(k):
        each_peer(lambda q: s3_copy(q, t, k).wait_send())

    all_sent(z)
    loop_planes(all_sent)
    loop_planes(lambda k: rs_copy(k, k, z, k).wait_send())


def local(ns, nt, qkv, conv_weight, decay_rate, residue, skip_gain, out_weight):
    tok, ch = qkv.shape[1], qkv.shape[2]
    modes = decay_rate.shape[0]
    groups = ch // LANES
    nz = ns // 2
    cols = out_weight.shape[1]
    rows = modes * groups
    decay = jnp.exp(-decay_rate).reshape(rows, LANES)
    decay_sec = jnp.exp(-decay_rate * tok).reshape(rows, LANES)
    gain = (residue * jnp.sqrt(-jnp.expm1(-2.0 * decay_rate))).reshape(rows, LANES)
    vmem = pl.BlockSpec(memory_space=pltpu.VMEM)
    f32, bf16 = jnp.float32, jnp.bfloat16
    dma = pltpu.SemaphoreType.DMA
    return pl.pallas_call(
        functools.partial(kernel, ns, nt, modes),
        out_shape=jax.ShapeDtypeStruct((tok, cols), bf16),
        in_specs=[vmem] * 6 + [pl.BlockSpec(memory_space=pl.ANY)],
        out_specs=vmem,
        scratch_shapes=[
            pltpu.VMEM((3, HALO, ch), bf16),
            pltpu.VMEM((3, HALO + tok, LANES), f32),
            pltpu.VMEM((tok * groups, LANES), f32),
            pltpu.VMEM((tok, ch), f32),
            pltpu.VMEM((tok, ch), bf16),
            pltpu.VMEM((ch, cols), bf16),
            pltpu.VMEM((rows, LANES), f32),
            pltpu.VMEM((rows, LANES), f32),
            pltpu.VMEM((rows, LANES), bf16),
            pltpu.VMEM((nz, rows, LANES), bf16),
            pltpu.VMEM((rows, LANES), f32),
            pltpu.VMEM((nt, tok // nt, ch), bf16),
            pltpu.VMEM((nz, tok, ch), bf16),
            pltpu.VMEM((nz, tok, cols), bf16),
            pltpu.VMEM((nz + 1, tok, cols), bf16),
            pltpu.VMEM((tok, cols), f32),
            dma((2,)),
            dma((3,)),
            dma((2,)),
            dma((nz,)),
            dma((nz,)),
            dma((nt,)),
            dma((nt,)),
            dma((nz,)),
            dma((nz,)),
            dma((nz, nt)),
            dma((nz, nt)),
            dma((nz,)),
            dma((nz + 1,)),
            dma((2,)),
        ],
        compiler_params=pltpu.CompilerParams(
            collective_id=0, has_side_effects=True, vmem_limit_bytes=56 * 1024 * 1024
        ),
        cost_estimate=pl.CostEstimate(
            flops=2 * tok * nz * ch * cols, bytes_accessed=12 * 1024 * 1024, transcendentals=0
        ),
    )(
        qkv,
        conv_weight.reshape(-1, ch),
        decay,
        decay_sec,
        gain,
        skip_gain.reshape(groups, LANES),
        out_weight,
    )


def solution(mesh):
    return jax.shard_map(
        functools.partial(local, mesh.shape["seq"], mesh.shape["tensor"]),
        mesh=mesh,
        in_specs=(
            P(None, "seq", "tensor"),
            P(None, None, "tensor"),
            P(None, "tensor"),
            P(None, "tensor"),
            P("tensor"),
            P("seq", "tensor"),
        ),
        out_specs=P("seq", "tensor"),
        check_vma=False,
    )
```

```python
import functools

import jax
import jax.numpy as jnp
from jax import lax
from jax.experimental import pallas as pl
from jax.experimental.pallas import tpu as pltpu
from jax.sharding import PartitionSpec as P

MESH = pl.DeviceIdType.MESH
LANES = 128
HALO = 16


def token_parts(tok, nt):
    return 2 if tok % (2 * nt * HALO) == 0 else 1


def one_minus_exp(x):
    small = jnp.ones_like(x)
    for n in range(9, 1, -1):
        small = 1.0 - small * x * (1.0 / n)
    return jnp.where(x < 0.25, x * small, 1.0 - jnp.exp(-x))


def kernel(
    ns,
    nt,
    modes,
    qkv,
    conv_w,
    rate,
    residue,
    skip_row,
    weight,
    out,
    decay,
    decay_sec,
    gain,
    skip,
    halo,
    ext,
    prod,
    qf,
    mixed,
    wfull,
    state,
    other,
    total,
    totals,
    enter,
    stage,
    full,
    part,
    recv,
    own,
    halo_sem,
    w_sem,
    swap_sem,
    tot_send,
    tot_recv,
    s1_send,
    s1_recv,
    s2_send,
    s2_recv,
    s3_send,
    s3_recv,
    rs_send,
    rs_recv,
):
    nz = ns // 2
    tok = qkv.shape[1]
    ch = qkv.shape[2]
    groups = ch // LANES
    parts = token_parts(tok, nt)
    rows_part = tok // parts
    piece = rows_part // nt
    width = min(8, groups)
    halves = groups // width
    span = modes * width
    rows_w = weight.shape[0]
    cols = weight.shape[1]
    s = lax.axis_index("seq")
    t = lax.axis_index("tensor")
    z = s // 2
    c = s % 2
    mate = 2 * z + (1 - c)

    def dev(seq, ten):
        return (seq, ten)

    barrier = pltpu.get_barrier_semaphore()
    for d in range(1, ns):
        pl.semaphore_signal(barrier, inc=1, device_id=dev((s + d) % ns, t), device_id_type=MESH)
    for d in range(1, nt):
        pl.semaphore_signal(barrier, inc=1, device_id=dev(s, (t + d) % nt), device_id_type=MESH)
    pl.semaphore_wait(barrier, ns - 1 + nt - 1)

    halo_copy = pltpu.make_async_remote_copy(
        src_ref=qkv.at[:, pl.ds(tok - HALO, HALO), :],
        dst_ref=halo,
        send_sem=halo_sem.at[0],
        recv_sem=halo_sem.at[1],
        device_id=dev((s + 1) % ns, t),
        device_id_type=MESH,
    )

    @pl.when(s < ns - 1)
    def _():
        halo_copy.start()

    w_rows = pl.ds(pl.multiple_of(c * rows_w, rows_w), rows_w)
    w_remote = pltpu.make_async_remote_copy(
        src_ref=weight,
        dst_ref=wfull.at[w_rows, :],
        send_sem=w_sem.at[0],
        recv_sem=w_sem.at[1],
        device_id=dev(mate, t),
        device_id_type=MESH,
    )
    w_remote.start()
    w_local = pltpu.make_async_copy(weight, wfull.at[w_rows, :], w_sem.at[2])
    w_local.start()

    for g in range(groups):
        lanes = pl.ds(g * LANES, LANES)
        rows = pl.ds((g // width) * span + g % width, modes, stride=width)
        r = rate[:, lanes]
        decay[rows, :] = jnp.exp(-r)
        decay_sec[rows, :] = jnp.exp(-r * tok)
        gain[rows, :] = residue[:, lanes] * jnp.sqrt(one_minus_exp(2.0 * r))
        skip[g : g + 1, :] = skip_row[:, lanes]

    @pl.when(s == 0)
    def _():
        halo[...] = jnp.zeros_like(halo)

    @pl.when(s > 0)
    def _():
        halo_copy.wait_recv()

    def short(i, lanes):
        ext[i, 0:HALO, :] = halo[i, :, lanes].astype(jnp.float32)
        ext[i, HALO : HALO + tok, :] = qkv[i, :, lanes].astype(jnp.float32)
        taps = conv_w[i, :, lanes]
        return (
            taps[0:1] * ext[i, HALO : HALO + tok, :]
            + taps[1:2] * ext[i, HALO - 1 : HALO - 1 + tok, :]
            + taps[2:3] * ext[i, HALO - 2 : HALO - 2 + tok, :]
        )

    def mode_rows(ref, m, h):
        return ref[h * span + m * width : h * span + (m + 1) * width, :]

    def half_rows(h):
        return pl.ds(h * span, span)

    def tree(values):
        while len(values) > 1:
            values = [a + b for a, b in zip(values[::2], values[1::2])] + (
                [values[-1]] if len(values) % 2 else []
            )
        return values[0]

    def keys_values(h):
        for g in range(h * width, (h + 1) * width):
            lanes = pl.ds(g * LANES, LANES)
            prod[pl.ds(g, tok, stride=groups), :] = short(1, lanes) * short(2, lanes)

    def queries(h):
        for g in range(h * width, (h + 1) * width):
            lanes = pl.ds(g * LANES, LANES)
            qf[:, lanes] = short(0, lanes)

    def recur(h):
        skips = skip[h * width : (h + 1) * width, :]

        def step(i, states):
            rows = pl.ds(pl.multiple_of(i * groups + h * width, width), width)
            x = prod[rows, :]
            new = tuple(st * mode_rows(decay, m, h) + x for m, st in enumerate(states))
            terms = [st * mode_rows(gain, m, h) for m, st in enumerate(new)]
            prod[rows, :] = tree(terms) + skips * x
            return new

        states = lax.fori_loop(
            0,
            tok,
            step,
            tuple(jnp.zeros((width, LANES), jnp.float32) for _ in range(modes)),
            unroll=4,
        )
        for m in range(modes):
            state[h * span + m * width : h * span + (m + 1) * width, :] = states[m]

    def swap(h):
        return pltpu.make_async_remote_copy(
            src_ref=state.at[half_rows(h), :],
            dst_ref=other.at[half_rows(h), :],
            send_sem=swap_sem.at[0, h],
            recv_sem=swap_sem.at[1, h],
            device_id=dev(mate, t),
            device_id_type=MESH,
        )

    def tot_copy(h, target, source):
        return pltpu.make_async_remote_copy(
            src_ref=total.at[half_rows(h), :],
            dst_ref=totals.at[source, half_rows(h), :],
            send_sem=tot_send.at[h, target],
            recv_sem=tot_recv.at[h, source],
            device_id=dev(2 * target + c, t),
            device_id_type=MESH,
        )

    def send_totals(h):
        rows = half_rows(h)
        swap(h).wait_recv()

        @pl.when(c == 0)
        def _():
            total[rows, :] = (decay_sec[rows, :] * state[rows, :] + other[rows, :]).astype(
                total.dtype
            )

        @pl.when(c == 1)
        def _():
            total[rows, :] = (decay_sec[rows, :] * other[rows, :] + state[rows, :]).astype(
                total.dtype
            )

        for k in range(1, nz):

            @pl.when(k > z)
            def _(k=k):
                tot_copy(h, k, z).start()

    def entering(h):
        rows = half_rows(h)
        enter[rows, :] = jnp.zeros((span, LANES), jnp.float32)
        for k in range(nz - 1):

            @pl.when(k < z)
            def _(k=k):
                tot_copy(h, z, k).wait_recv()
                both = decay_sec[rows, :] * decay_sec[rows, :]
                enter[rows, :] = enter[rows, :] * both + totals[k, rows, :].astype(jnp.float32)

        @pl.when(c == 1)
        def _():
            enter[rows, :] = decay_sec[rows, :] * enter[rows, :] + other[rows, :]

    def fix(h):
        def step(i, carried):
            rows = pl.ds(pl.multiple_of(i * groups + h * width, width), width)
            prod[rows, :] = prod[rows, :] + tree(list(carried))
            return tuple(u * mode_rows(decay, m, h) for m, u in enumerate(carried))

        lax.fori_loop(
            0,
            tok,
            step,
            tuple(
                mode_rows(gain, m, h) * mode_rows(decay, m, h) * mode_rows(enter, m, h)
                for m in range(modes)
            ),
            unroll=4,
        )
        for g in range(h * width, (h + 1) * width):
            lanes = pl.ds(g * LANES, LANES)
            mixed[:, lanes] = (qf[:, lanes] * prod[pl.ds(g, tok, stride=groups), :]).astype(
                mixed.dtype
            )

    def share(p, index):
        return pl.ds(pl.multiple_of(p * rows_part + index * piece, piece), piece)

    def half_lanes(h):
        return pl.ds(h * width * LANES, width * LANES)

    def s1_copy(h, p, target, source):
        return pltpu.make_async_remote_copy(
            src_ref=mixed.at[share(p, target), half_lanes(h)],
            dst_ref=stage.at[p, source, :, half_lanes(h)],
            send_sem=s1_send.at[h, p, target],
            recv_sem=s1_recv.at[h, p, source],
            device_id=dev(s, target),
            device_id_type=MESH,
        )

    def s1_local(h, p):
        return pltpu.make_async_copy(
            mixed.at[share(p, t), half_lanes(h)],
            stage.at[p, t, :, half_lanes(h)],
            s1_recv.at[h, p, t],
        )

    def each_peer(body):
        def one(d, carry):
            body((t + d) % nt)
            return carry

        lax.fori_loop(1, nt, one, 0)

    def scatter(h):
        for p in range(parts):
            each_peer(lambda q: s1_copy(h, p, q, t).start())
            s1_local(h, p).start()

    def scattered(h, p, k):
        @pl.when(k == t)
        def _():
            s1_local(h, p).wait()

        @pl.when(k != t)
        def _():
            s1_copy(h, p, t, k).wait_recv()

    for h in range(halves):
        keys_values(h)
        if h > 0:
            send_totals(h - 1)
        recur(h)
        swap(h).start()
    queries(0)
    send_totals(halves - 1)
    for h in range(halves):
        if h > 0:
            queries(h)
        entering(h)
        fix(h)
        scatter(h)

    def s2_copy(h, p, target, source):
        return pltpu.make_async_remote_copy(
            src_ref=stage.at[p, target, :, half_lanes(h)],
            dst_ref=full.at[source, share(p, t), half_lanes(h)],
            send_sem=s2_send.at[h, p, target],
            recv_sem=s2_recv.at[h, p, source],
            device_id=dev(2 * target + c, t),
            device_id_type=MESH,
        )

    def s2_local(h, p):
        return pltpu.make_async_copy(
            stage.at[p, z, :, half_lanes(h)],
            full.at[z, share(p, t), half_lanes(h)],
            s2_recv.at[h, p, z],
        )

    candidates = 2 * (nz - 1) * parts

    def each_plane(f, body):
        p = f % parts
        e = f // parts
        d = nz - 1 - e // 2
        k = z + d * (1 - 2 * (e % 2))

        @pl.when((k >= 0) & (k < nz))
        def _():
            body(k, p)

    def loop_planes(body):
        def one(f, carry):
            each_plane(f, body)
            return carry

        lax.fori_loop(0, candidates, one, 0)

    for h in range(halves):

        def go(k, p, h=h):
            scattered(h, p, k)
            s2_copy(h, p, k, z).start()

        loop_planes(go)
        for p in range(parts):
            scattered(h, p, z)
            s2_local(h, p).start()

    def s3_copy(target, source, k, p):
        rows = full.at[k, share(p, source), :]
        return pltpu.make_async_remote_copy(
            src_ref=rows,
            dst_ref=rows,
            send_sem=s3_send.at[k * parts + p, target],
            recv_sem=s3_recv.at[k * parts + p, source],
            device_id=dev(s, target),
            device_id_type=MESH,
        )

    def spread(k, p):
        each_peer(lambda q: s3_copy(q, t, k, p).start())

    def spread_received(k, p):
        for h in range(halves):
            s2_copy(h, p, z, k).wait_recv()
        spread(k, p)

    def gathered(k, p):
        each_peer(lambda q: s3_copy(t, q, k, p).wait_recv())

    tile = min(512, cols)

    def part_rows(p):
        return pl.ds(pl.multiple_of(p * rows_part, rows_part), rows_part)

    def product(k, p, store):
        def one(n, carry):
            lanes = pl.ds(pl.multiple_of(n * tile, tile), tile)
            store(
                lanes,
                jnp.dot(
                    full[k, part_rows(p), :],
                    wfull[:, lanes],
                    preferred_element_type=jnp.float32,
                ),
            )
            return carry

        lax.fori_loop(0, cols // tile, one, 0)

    def rs_copy(k, p, slot, target):
        return pltpu.make_async_remote_copy(
            src_ref=part.at[k, part_rows(p), :],
            dst_ref=recv.at[slot, part_rows(p), :],
            send_sem=rs_send.at[k, p],
            recv_sem=rs_recv.at[slot, p],
            device_id=dev(2 * target + c, t),
            device_id_type=MESH,
        )

    def rs_wait(slot, p):
        rs_copy(z, p, slot, z).wait_recv()

    def contribute(k, p):
        gathered(k, p)
        rows = part_rows(p)

        def fresh(lanes, value):
            part[k, rows, lanes] = value.astype(part.dtype)

        def added(lanes, value):
            part[k, rows, lanes] = (value + recv[k, rows, lanes].astype(jnp.float32)).astype(
                part.dtype
            )

        first = ((k > z) & (z == 0)) | ((k < z) & (z == nz - 1))

        @pl.when(first)
        def _():
            product(k, p, fresh)

        @pl.when(jnp.logical_not(first))
        def _():
            rs_wait(k, p)
            product(k, p, added)

        @pl.when(k > z)
        def _():
            rs_copy(k, p, k, z + 1).start()

        @pl.when(k < z - 1)
        def _():
            rs_copy(k, p, k, z - 1).start()

        @pl.when(k == z - 1)
        def _():
            rs_copy(k, p, nz, z - 1).start()

    lead = parts
    for f in range(lead):
        each_plane(f, spread_received)
    for p in range(parts):
        for h in range(halves):
            s2_local(h, p).wait()
        spread(z, p)
    w_local.wait()
    w_remote.wait_recv()

    def one_plane(f, carry):
        @pl.when(f + lead < candidates)
        def _():
            each_plane(f + lead, spread_received)

        each_plane(f, contribute)
        return carry

    lax.fori_loop(0, candidates, one_plane, 0)

    for p in range(parts):
        gathered(z, p)

        def keep_own(lanes, value, p=p):
            own[part_rows(p), lanes] = value

        product(z, p, keep_own)

    for p in range(parts):
        rows = part_rows(p)

        @pl.when(z > 0)
        def _(p=p, rows=rows):
            rs_wait(z, p)
            own[rows, :] += recv[z, rows, :].astype(jnp.float32)

        @pl.when(z < nz - 1)
        def _(p=p, rows=rows):
            rs_wait(nz, p)
            own[rows, :] += recv[nz, rows, :].astype(jnp.float32)

        out[rows, :] = own[rows, :].astype(out.dtype)

    @pl.when(s < ns - 1)
    def _():
        halo_copy.wait_send()

    w_remote.wait_send()
    for h in range(halves):
        swap(h).wait_send()
        for k in range(1, nz):

            @pl.when(k > z)
            def _(k=k, h=h):
                tot_copy(h, k, z).wait_send()

        for p in range(parts):
            each_peer(lambda q, h=h, p=p: s1_copy(h, p, q, t).wait_send())
        loop_planes(lambda k, p, h=h: s2_copy(h, p, k, z).wait_send())

    def all_sent(k, p):
        each_peer(lambda q: s3_copy(q, t, k, p).wait_send())

    for p in range(parts):
        all_sent(z, p)
    loop_planes(all_sent)
    loop_planes(lambda k, p: rs_copy(k, p, k, z).wait_send())


def local(ns, nt, qkv, conv_weight, decay_rate, residue, skip_gain, out_weight):
    tok, ch = qkv.shape[1], qkv.shape[2]
    modes = decay_rate.shape[0]
    groups = ch // LANES
    nz = ns // 2
    cols = out_weight.shape[1]
    rows = modes * groups
    parts = token_parts(tok, nt)
    halves = groups // min(8, groups)
    vmem = pl.BlockSpec(memory_space=pltpu.VMEM)
    f32, bf16 = jnp.float32, jnp.bfloat16
    dma = pltpu.SemaphoreType.DMA
    return pl.pallas_call(
        functools.partial(kernel, ns, nt, modes),
        out_shape=jax.ShapeDtypeStruct((tok, cols), bf16),
        in_specs=[vmem] * 5 + [pl.BlockSpec(memory_space=pl.ANY)],
        out_specs=vmem,
        scratch_shapes=[
            pltpu.VMEM((rows, LANES), f32),
            pltpu.VMEM((rows, LANES), f32),
            pltpu.VMEM((rows, LANES), f32),
            pltpu.VMEM((groups, LANES), f32),
            pltpu.VMEM((3, HALO, ch), bf16),
            pltpu.VMEM((3, HALO + tok, LANES), f32),
            pltpu.VMEM((tok * groups, LANES), f32),
            pltpu.VMEM((tok, ch), f32),
            pltpu.VMEM((tok, ch), bf16),
            pltpu.VMEM((ch, cols), bf16),
            pltpu.VMEM((rows, LANES), f32),
            pltpu.VMEM((rows, LANES), f32),
            pltpu.VMEM((rows, LANES), bf16),
            pltpu.VMEM((nz, rows, LANES), bf16),
            pltpu.VMEM((rows, LANES), f32),
            pltpu.VMEM((parts, nt, tok // parts // nt, ch), bf16),
            pltpu.VMEM((nz, tok, ch), bf16),
            pltpu.VMEM((nz, tok, cols), bf16),
            pltpu.VMEM((nz + 1, tok, cols), bf16),
            pltpu.VMEM((tok, cols), f32),
            dma((2,)),
            dma((3,)),
            dma((2, halves)),
            dma((halves, nz)),
            dma((halves, nz)),
            dma((halves, parts, nt)),
            dma((halves, parts, nt)),
            dma((halves, parts, nz)),
            dma((halves, parts, nz)),
            dma((nz * parts, nt)),
            dma((nz * parts, nt)),
            dma((nz, parts)),
            dma((nz + 1, parts)),
        ],
        compiler_params=pltpu.CompilerParams(
            collective_id=0, has_side_effects=True, vmem_limit_bytes=56 * 1024 * 1024
        ),
        cost_estimate=pl.CostEstimate(
            flops=2 * tok * nz * ch * cols, bytes_accessed=12 * 1024 * 1024, transcendentals=0
        ),
    )(
        qkv,
        conv_weight,
        decay_rate,
        residue,
        skip_gain.reshape(1, ch),
        out_weight,
    )


def solution(mesh):
    return jax.shard_map(
        functools.partial(local, mesh.shape["seq"], mesh.shape["tensor"]),
        mesh=mesh,
        in_specs=(
            P(None, "seq", "tensor"),
            P(None, None, "tensor"),
            P(None, "tensor"),
            P(None, "tensor"),
            P("tensor"),
            P("seq", "tensor"),
        ),
        out_specs=P("seq", "tensor"),
        check_vma=False,
    )
```

```python
import functools

import jax
import jax.numpy as jnp
from jax import lax
from jax.experimental import pallas as pl
from jax.experimental.pallas import tpu as pltpu
from jax.sharding import PartitionSpec as P

MESH = pl.DeviceIdType.MESH
LANES = 128
HALO = 16


def token_parts(tok, nt):
    return 2 if tok % (2 * nt * HALO) == 0 else 1


def one_minus_exp(x):
    small = jnp.ones_like(x)
    for n in range(9, 1, -1):
        small = 1.0 - small * x * (1.0 / n)
    return jnp.where(x < 0.25, x * small, 1.0 - jnp.exp(-x))


def kernel(
    ns,
    nt,
    modes,
    qkv,
    conv_w,
    rate,
    residue,
    skip_row,
    weight,
    out,
    decay,
    decay_sec,
    gain,
    skip,
    halo,
    ext,
    prod,
    qf,
    mixed,
    wfull,
    state,
    other,
    total,
    totals,
    enter,
    stage,
    full,
    part,
    recv,
    own,
    halo_sem,
    w_sem,
    swap_sem,
    tot_send,
    tot_recv,
    s1_send,
    s1_recv,
    s2_send,
    s2_recv,
    s3_send,
    s3_recv,
    rs_send,
    rs_recv,
):
    nz = ns // 2
    tok = qkv.shape[1]
    ch = qkv.shape[2]
    groups = ch // LANES
    parts = token_parts(tok, nt)
    rows_part = tok // parts
    piece = rows_part // nt
    width = min(8, groups)
    halves = groups // width
    span = modes * width
    rows_w = weight.shape[0]
    cols = weight.shape[1]
    s = lax.axis_index("seq")
    t = lax.axis_index("tensor")
    z = s // 2
    c = s % 2
    mate = 2 * z + (1 - c)

    def dev(seq, ten):
        return (seq, ten)

    barrier = pltpu.get_barrier_semaphore()
    for d in range(1, ns):
        pl.semaphore_signal(barrier, inc=1, device_id=dev((s + d) % ns, t), device_id_type=MESH)
    for d in range(1, nt):
        pl.semaphore_signal(barrier, inc=1, device_id=dev(s, (t + d) % nt), device_id_type=MESH)

    halo_copy = pltpu.make_async_remote_copy(
        src_ref=qkv.at[:, pl.ds(tok - HALO, HALO), :],
        dst_ref=halo,
        send_sem=halo_sem.at[0],
        recv_sem=halo_sem.at[1],
        device_id=dev((s + 1) % ns, t),
        device_id_type=MESH,
    )

    w_rows = pl.ds(pl.multiple_of(c * rows_w, rows_w), rows_w)
    w_remote = pltpu.make_async_remote_copy(
        src_ref=weight,
        dst_ref=wfull.at[w_rows, :],
        send_sem=w_sem.at[0],
        recv_sem=w_sem.at[1],
        device_id=dev(mate, t),
        device_id_type=MESH,
    )
    w_local = pltpu.make_async_copy(weight, wfull.at[w_rows, :], w_sem.at[2])

    def short(i, lanes, head, count):
        ext[i, 0:HALO, :] = head
        ext[i, HALO : HALO + count, :] = qkv[i, 0:count, lanes].astype(jnp.float32)
        taps = conv_w[i, :, lanes]
        return (
            taps[0:1] * ext[i, HALO : HALO + count, :]
            + taps[1:2] * ext[i, HALO - 1 : HALO - 1 + count, :]
            + taps[2:3] * ext[i, HALO - 2 : HALO - 2 + count, :]
        )

    def before(i, lanes):
        return halo[i, :, lanes].astype(jnp.float32)

    def mode_rows(ref, m, h):
        return ref[h * span + m * width : h * span + (m + 1) * width, :]

    def half_rows(h):
        return pl.ds(h * span, span)

    def tree(values):
        while len(values) > 1:
            values = [a + b for a, b in zip(values[::2], values[1::2])] + (
                [values[-1]] if len(values) % 2 else []
            )
        return values[0]

    def keys_values(h):
        zero = jnp.zeros((HALO, LANES), jnp.float32)
        for g in range(h * width, (h + 1) * width):
            lanes = pl.ds(g * LANES, LANES)
            prod[pl.ds(g, tok, stride=groups), :] = short(1, lanes, zero, tok) * short(
                2, lanes, zero, tok
            )

    def first_rows(h):
        for g in range(h * width, (h + 1) * width):
            lanes = pl.ds(g * LANES, LANES)
            prod[pl.ds(g, HALO, stride=groups), :] = short(
                1, lanes, before(1, lanes), HALO
            ) * short(2, lanes, before(2, lanes), HALO)

    def queries(h):
        for g in range(h * width, (h + 1) * width):
            lanes = pl.ds(g * LANES, LANES)
            qf[:, lanes] = short(0, lanes, before(0, lanes), tok)

    def recur(h):
        skips = skip[h * width : (h + 1) * width, :]

        def step(i, states):
            rows = pl.ds(pl.multiple_of(i * groups + h * width, width), width)
            x = prod[rows, :]
            new = tuple(st * mode_rows(decay, m, h) + x for m, st in enumerate(states))
            terms = [st * mode_rows(gain, m, h) for m, st in enumerate(new)]
            prod[rows, :] = tree(terms) + skips * x
            return new

        states = lax.fori_loop(
            0,
            tok,
            step,
            tuple(jnp.zeros((width, LANES), jnp.float32) for _ in range(modes)),
            unroll=4,
        )
        for m in range(modes):
            state[h * span + m * width : h * span + (m + 1) * width, :] = states[m]

    def swap(h):
        return pltpu.make_async_remote_copy(
            src_ref=state.at[half_rows(h), :],
            dst_ref=other.at[half_rows(h), :],
            send_sem=swap_sem.at[0, h],
            recv_sem=swap_sem.at[1, h],
            device_id=dev(mate, t),
            device_id_type=MESH,
        )

    def tot_copy(h, target, source):
        return pltpu.make_async_remote_copy(
            src_ref=total.at[half_rows(h), :],
            dst_ref=totals.at[source, half_rows(h), :],
            send_sem=tot_send.at[h, target],
            recv_sem=tot_recv.at[h, source],
            device_id=dev(2 * target + c, t),
            device_id_type=MESH,
        )

    def send_totals(h):
        rows = half_rows(h)
        swap(h).wait_recv()

        @pl.when(c == 0)
        def _():
            total[rows, :] = (decay_sec[rows, :] * state[rows, :] + other[rows, :]).astype(
                total.dtype
            )

        @pl.when(c == 1)
        def _():
            total[rows, :] = (decay_sec[rows, :] * other[rows, :] + state[rows, :]).astype(
                total.dtype
            )

        for k in range(1, nz):

            @pl.when(k > z)
            def _(k=k):
                tot_copy(h, k, z).start()

    def entering(h):
        rows = half_rows(h)
        enter[rows, :] = jnp.zeros((span, LANES), jnp.float32)
        for k in range(nz - 1):

            @pl.when(k < z)
            def _(k=k):
                tot_copy(h, z, k).wait_recv()
                both = decay_sec[rows, :] * decay_sec[rows, :]
                enter[rows, :] = enter[rows, :] * both + totals[k, rows, :].astype(jnp.float32)

        @pl.when(c == 1)
        def _():
            enter[rows, :] = decay_sec[rows, :] * enter[rows, :] + other[rows, :]

    def fix(h):
        def step(i, carried):
            rows = pl.ds(pl.multiple_of(i * groups + h * width, width), width)
            prod[rows, :] = prod[rows, :] + tree(list(carried))
            return tuple(u * mode_rows(decay, m, h) for m, u in enumerate(carried))

        lax.fori_loop(
            0,
            tok,
            step,
            tuple(
                mode_rows(gain, m, h) * mode_rows(decay, m, h) * mode_rows(enter, m, h)
                for m in range(modes)
            ),
            unroll=4,
        )
        for g in range(h * width, (h + 1) * width):
            lanes = pl.ds(g * LANES, LANES)
            mixed[:, lanes] = (qf[:, lanes] * prod[pl.ds(g, tok, stride=groups), :]).astype(
                mixed.dtype
            )

    def share(p, index):
        return pl.ds(pl.multiple_of(p * rows_part + index * piece, piece), piece)

    def half_lanes(h):
        return pl.ds(h * width * LANES, width * LANES)

    def s1_copy(h, p, target, source):
        return pltpu.make_async_remote_copy(
            src_ref=mixed.at[share(p, target), half_lanes(h)],
            dst_ref=stage.at[p, source, :, half_lanes(h)],
            send_sem=s1_send.at[h, p, target],
            recv_sem=s1_recv.at[h, p, source],
            device_id=dev(s, target),
            device_id_type=MESH,
        )

    def s1_local(h, p):
        return pltpu.make_async_copy(
            mixed.at[share(p, t), half_lanes(h)],
            stage.at[p, t, :, half_lanes(h)],
            s1_recv.at[h, p, t],
        )

    def each_peer(body):
        def one(d, carry):
            body((t + d) % nt)
            return carry

        lax.fori_loop(1, nt, one, 0)

    def scatter(h):
        for p in range(parts):
            each_peer(lambda q: s1_copy(h, p, q, t).start())
            s1_local(h, p).start()

    def scattered(h, p, k):
        @pl.when(k == t)
        def _():
            s1_local(h, p).wait()

        @pl.when(k != t)
        def _():
            s1_copy(h, p, t, k).wait_recv()

    def s2_copy(h, p, target, source):
        return pltpu.make_async_remote_copy(
            src_ref=stage.at[p, target, :, half_lanes(h)],
            dst_ref=full.at[source, share(p, t), half_lanes(h)],
            send_sem=s2_send.at[h, p, target],
            recv_sem=s2_recv.at[h, p, source],
            device_id=dev(2 * target + c, t),
            device_id_type=MESH,
        )

    def s2_local(h, p):
        return pltpu.make_async_copy(
            stage.at[p, z, :, half_lanes(h)],
            full.at[z, share(p, t), half_lanes(h)],
            s2_recv.at[h, p, z],
        )

    candidates = 2 * (nz - 1) * parts

    def each_plane(f, body):
        p = (f // 2) % parts
        d = nz - 1 - f // (2 * parts)
        k = z + d * (1 - 2 * (f % 2))

        @pl.when((k >= 0) & (k < nz))
        def _():
            body(k, p)

    def loop_planes(body):
        def one(f, carry):
            each_plane(f, body)
            return carry

        lax.fori_loop(0, candidates, one, 0)

    def to_planes(h):
        def go(k, p):
            scattered(h, p, k)
            s2_copy(h, p, k, z).start()

        loop_planes(go)
        for p in range(parts):
            scattered(h, p, z)
            s2_local(h, p).start()

    for g in range(groups):
        lanes = pl.ds(g * LANES, LANES)
        rows = pl.ds((g // width) * span + g % width, modes, stride=width)
        r = rate[:, lanes]
        decay[rows, :] = jnp.exp(-r)
        decay_sec[rows, :] = jnp.exp(-r * tok)
        gain[rows, :] = residue[:, lanes] * jnp.sqrt(one_minus_exp(2.0 * r))
        skip[g : g + 1, :] = skip_row[:, lanes]

    keys_values(0)
    pl.semaphore_wait(barrier, ns - 1 + nt - 1)

    @pl.when(s < ns - 1)
    def _():
        halo_copy.start()

    w_remote.start()
    w_local.start()

    @pl.when(s == 0)
    def _():
        halo[...] = jnp.zeros_like(halo)

    @pl.when(s > 0)
    def _():
        halo_copy.wait_recv()

    first_rows(0)
    recur(0)
    swap(0).start()
    for h in range(halves):
        if h + 1 < halves:
            keys_values(h + 1)
            first_rows(h + 1)
        else:
            queries(h)
        send_totals(h)
        if h > 0:
            to_planes(h - 1)
        if h + 1 < halves:
            queries(h)
        entering(h)
        fix(h)
        scatter(h)
        if h + 1 < halves:
            recur(h + 1)
            swap(h + 1).start()
    to_planes(halves - 1)

    def s3_copy(target, source, k, p):
        rows = full.at[k, share(p, source), :]
        return pltpu.make_async_remote_copy(
            src_ref=rows,
            dst_ref=rows,
            send_sem=s3_send.at[k * parts + p, target],
            recv_sem=s3_recv.at[k * parts + p, source],
            device_id=dev(s, target),
            device_id_type=MESH,
        )

    def spread(k, p):
        each_peer(lambda q: s3_copy(q, t, k, p).start())

    def spread_received(k, p):
        for h in range(halves):
            s2_copy(h, p, z, k).wait_recv()
        spread(k, p)

    def gathered(k, p):
        each_peer(lambda q: s3_copy(t, q, k, p).wait_recv())

    tile = min(512, cols)

    def part_rows(p):
        return pl.ds(pl.multiple_of(p * rows_part, rows_part), rows_part)

    def product(k, p, store):
        def one(n, carry):
            lanes = pl.ds(pl.multiple_of(n * tile, tile), tile)
            store(
                lanes,
                jnp.dot(
                    full[k, part_rows(p), :],
                    wfull[:, lanes],
                    preferred_element_type=jnp.float32,
                ),
            )
            return carry

        lax.fori_loop(0, cols // tile, one, 0)

    def rs_copy(k, p, slot, target):
        return pltpu.make_async_remote_copy(
            src_ref=part.at[k, part_rows(p), :],
            dst_ref=recv.at[slot, part_rows(p), :],
            send_sem=rs_send.at[k, p],
            recv_sem=rs_recv.at[slot, p],
            device_id=dev(2 * target + c, t),
            device_id_type=MESH,
        )

    def rs_wait(slot, p):
        rs_copy(z, p, slot, z).wait_recv()

    def contribute(k, p):
        gathered(k, p)
        rows = part_rows(p)

        def fresh(lanes, value):
            part[k, rows, lanes] = value.astype(part.dtype)

        def added(lanes, value):
            part[k, rows, lanes] = (value + recv[k, rows, lanes].astype(jnp.float32)).astype(
                part.dtype
            )

        first = ((k > z) & (z == 0)) | ((k < z) & (z == nz - 1))

        @pl.when(first)
        def _():
            product(k, p, fresh)

        @pl.when(jnp.logical_not(first))
        def _():
            rs_wait(k, p)
            product(k, p, added)

        @pl.when(k > z)
        def _():
            rs_copy(k, p, k, z + 1).start()

        @pl.when(k < z - 1)
        def _():
            rs_copy(k, p, k, z - 1).start()

        @pl.when(k == z - 1)
        def _():
            rs_copy(k, p, nz, z - 1).start()

    lead = 2
    for f in range(lead):
        each_plane(f, spread_received)
    for p in range(parts):
        for h in range(halves):
            s2_local(h, p).wait()
        spread(z, p)
    w_local.wait()
    w_remote.wait_recv()

    def one_plane(f, carry):
        @pl.when(f + lead < candidates)
        def _():
            each_plane(f + lead, spread_received)

        each_plane(f, contribute)
        return carry

    lax.fori_loop(0, candidates, one_plane, 0)

    for p in range(parts):
        gathered(z, p)

        def keep_own(lanes, value, p=p):
            own[part_rows(p), lanes] = value

        product(z, p, keep_own)

    for p in range(parts):
        rows = part_rows(p)

        @pl.when(z > 0)
        def _(p=p, rows=rows):
            rs_wait(z, p)
            own[rows, :] += recv[z, rows, :].astype(jnp.float32)

        @pl.when(z < nz - 1)
        def _(p=p, rows=rows):
            rs_wait(nz, p)
            own[rows, :] += recv[nz, rows, :].astype(jnp.float32)

        out[rows, :] = own[rows, :].astype(out.dtype)

    @pl.when(s < ns - 1)
    def _():
        halo_copy.wait_send()

    w_remote.wait_send()
    for h in range(halves):
        swap(h).wait_send()
        for k in range(1, nz):

            @pl.when(k > z)
            def _(k=k, h=h):
                tot_copy(h, k, z).wait_send()

        for p in range(parts):
            each_peer(lambda q, h=h, p=p: s1_copy(h, p, q, t).wait_send())
        loop_planes(lambda k, p, h=h: s2_copy(h, p, k, z).wait_send())

    def all_sent(k, p):
        each_peer(lambda q: s3_copy(q, t, k, p).wait_send())

    for p in range(parts):
        all_sent(z, p)
    loop_planes(all_sent)
    loop_planes(lambda k, p: rs_copy(k, p, k, z).wait_send())


def local(ns, nt, qkv, conv_weight, decay_rate, residue, skip_gain, out_weight):
    tok, ch = qkv.shape[1], qkv.shape[2]
    modes = decay_rate.shape[0]
    groups = ch // LANES
    nz = ns // 2
    cols = out_weight.shape[1]
    rows = modes * groups
    parts = token_parts(tok, nt)
    halves = groups // min(8, groups)
    vmem = pl.BlockSpec(memory_space=pltpu.VMEM)
    f32, bf16 = jnp.float32, jnp.bfloat16
    dma = pltpu.SemaphoreType.DMA
    return pl.pallas_call(
        functools.partial(kernel, ns, nt, modes),
        out_shape=jax.ShapeDtypeStruct((tok, cols), bf16),
        in_specs=[vmem] * 5 + [pl.BlockSpec(memory_space=pl.ANY)],
        out_specs=vmem,
        scratch_shapes=[
            pltpu.VMEM((rows, LANES), f32),
            pltpu.VMEM((rows, LANES), f32),
            pltpu.VMEM((rows, LANES), f32),
            pltpu.VMEM((groups, LANES), f32),
            pltpu.VMEM((3, HALO, ch), bf16),
            pltpu.VMEM((3, HALO + tok, LANES), f32),
            pltpu.VMEM((tok * groups, LANES), f32),
            pltpu.VMEM((tok, ch), f32),
            pltpu.VMEM((tok, ch), bf16),
            pltpu.VMEM((ch, cols), bf16),
            pltpu.VMEM((rows, LANES), f32),
            pltpu.VMEM((rows, LANES), f32),
            pltpu.VMEM((rows, LANES), bf16),
            pltpu.VMEM((nz, rows, LANES), bf16),
            pltpu.VMEM((rows, LANES), f32),
            pltpu.VMEM((parts, nt, tok // parts // nt, ch), bf16),
            pltpu.VMEM((nz, tok, ch), bf16),
            pltpu.VMEM((nz, tok, cols), bf16),
            pltpu.VMEM((nz + 1, tok, cols), bf16),
            pltpu.VMEM((tok, cols), f32),
            dma((2,)),
            dma((3,)),
            dma((2, halves)),
            dma((halves, nz)),
            dma((halves, nz)),
            dma((halves, parts, nt)),
            dma((halves, parts, nt)),
            dma((halves, parts, nz)),
            dma((halves, parts, nz)),
            dma((nz * parts, nt)),
            dma((nz * parts, nt)),
            dma((nz, parts)),
            dma((nz + 1, parts)),
        ],
        compiler_params=pltpu.CompilerParams(
            collective_id=0, has_side_effects=True, vmem_limit_bytes=56 * 1024 * 1024
        ),
        cost_estimate=pl.CostEstimate(
            flops=2 * tok * nz * ch * cols, bytes_accessed=12 * 1024 * 1024, transcendentals=0
        ),
    )(
        qkv,
        conv_weight,
        decay_rate,
        residue,
        skip_gain.reshape(1, ch),
        out_weight,
    )


def solution(mesh):
    return jax.shard_map(
        functools.partial(local, mesh.shape["seq"], mesh.shape["tensor"]),
        mesh=mesh,
        in_specs=(
            P(None, "seq", "tensor"),
            P(None, None, "tensor"),
            P(None, "tensor"),
            P(None, "tensor"),
            P("tensor"),
            P("seq", "tensor"),
        ),
        out_specs=P("seq", "tensor"),
        check_vma=False,
    )
```

```python
import functools

import jax
import jax.numpy as jnp
from jax import lax
from jax.experimental import pallas as pl
from jax.experimental.pallas import tpu as pltpu
from jax.sharding import PartitionSpec as P

MESH = pl.DeviceIdType.MESH
LANES = 128
HALO = 16


def token_parts(tok, nt):
    return 2 if tok % (2 * nt * HALO) == 0 else 1


def one_minus_exp(x):
    small = jnp.ones_like(x)
    for n in range(9, 1, -1):
        small = 1.0 - small * x * (1.0 / n)
    return jnp.where(x < 0.25, x * small, 1.0 - jnp.exp(-x))


def kernel(
    ns,
    nt,
    modes,
    qkv,
    conv_w,
    rate,
    residue,
    skip_row,
    weight,
    out,
    decay,
    decay_sec,
    gain,
    skip,
    halo,
    ext,
    prod,
    qf,
    mixed,
    wfull,
    state,
    other,
    total,
    totals,
    enter,
    stage,
    full,
    part,
    recv,
    own,
    halo_sem,
    w_sem,
    swap_sem,
    tot_send,
    tot_recv,
    s1_send,
    s1_recv,
    s2_send,
    s2_recv,
    s3_send,
    s3_recv,
    rs_send,
    rs_recv,
):
    nz = ns // 2
    tok = qkv.shape[1]
    ch = qkv.shape[2]
    groups = ch // LANES
    parts = token_parts(tok, nt)
    rows_part = tok // parts
    piece = rows_part // nt
    width = min(8, groups)
    halves = groups // width
    span = modes * width
    rows_w = weight.shape[0]
    cols = weight.shape[1]
    s = lax.axis_index("seq")
    t = lax.axis_index("tensor")
    z = s // 2
    c = s % 2
    mate = 2 * z + (1 - c)

    def dev(seq, ten):
        return (seq, ten)

    barrier = pltpu.get_barrier_semaphore()
    for d in range(1, ns):
        pl.semaphore_signal(barrier, inc=1, device_id=dev((s + d) % ns, t), device_id_type=MESH)
    for d in range(1, nt):
        pl.semaphore_signal(barrier, inc=1, device_id=dev(s, (t + d) % nt), device_id_type=MESH)

    halo_copy = pltpu.make_async_remote_copy(
        src_ref=qkv.at[:, pl.ds(tok - HALO, HALO), :],
        dst_ref=halo,
        send_sem=halo_sem.at[0],
        recv_sem=halo_sem.at[1],
        device_id=dev((s + 1) % ns, t),
        device_id_type=MESH,
    )

    w_rows = pl.ds(pl.multiple_of(c * rows_w, rows_w), rows_w)
    w_remote = pltpu.make_async_remote_copy(
        src_ref=weight,
        dst_ref=wfull.at[w_rows, :],
        send_sem=w_sem.at[0],
        recv_sem=w_sem.at[1],
        device_id=dev(mate, t),
        device_id_type=MESH,
    )
    w_local = pltpu.make_async_copy(weight, wfull.at[w_rows, :], w_sem.at[2])

    def short(i, lanes, head, count):
        ext[i, 0:HALO, :] = head
        ext[i, HALO : HALO + count, :] = qkv[i, 0:count, lanes].astype(jnp.float32)
        taps = conv_w[i, :, lanes]
        return (
            taps[0:1] * ext[i, HALO : HALO + count, :]
            + taps[1:2] * ext[i, HALO - 1 : HALO - 1 + count, :]
            + taps[2:3] * ext[i, HALO - 2 : HALO - 2 + count, :]
        )

    def before(i, lanes):
        return halo[i, :, lanes].astype(jnp.float32)

    def mode_rows(ref, m, h):
        return ref[h * span + m * width : h * span + (m + 1) * width, :]

    def half_rows(h):
        return pl.ds(h * span, span)

    def tree(values):
        while len(values) > 1:
            values = [a + b for a, b in zip(values[::2], values[1::2])] + (
                [values[-1]] if len(values) % 2 else []
            )
        return values[0]

    def keys_values(h):
        zero = jnp.zeros((HALO, LANES), jnp.float32)
        for g in range(h * width, (h + 1) * width):
            lanes = pl.ds(g * LANES, LANES)
            prod[pl.ds(g, tok, stride=groups), :] = short(1, lanes, zero, tok) * short(
                2, lanes, zero, tok
            )

    def first_rows(h):
        for g in range(h * width, (h + 1) * width):
            lanes = pl.ds(g * LANES, LANES)
            prod[pl.ds(g, HALO, stride=groups), :] = short(
                1, lanes, before(1, lanes), HALO
            ) * short(2, lanes, before(2, lanes), HALO)

    def queries(h):
        for g in range(h * width, (h + 1) * width):
            lanes = pl.ds(g * LANES, LANES)
            qf[:, lanes] = short(0, lanes, before(0, lanes), tok)

    def recur(h):
        skips = skip[h * width : (h + 1) * width, :]

        def step(i, states):
            rows = pl.ds(pl.multiple_of(i * groups + h * width, width), width)
            x = prod[rows, :]
            new = tuple(st * mode_rows(decay, m, h) + x for m, st in enumerate(states))
            terms = [st * mode_rows(gain, m, h) for m, st in enumerate(new)]
            prod[rows, :] = tree(terms) + skips * x
            return new

        states = lax.fori_loop(
            0,
            tok,
            step,
            tuple(jnp.zeros((width, LANES), jnp.float32) for _ in range(modes)),
            unroll=4,
        )
        for m in range(modes):
            state[h * span + m * width : h * span + (m + 1) * width, :] = states[m]

    def swap(h):
        return pltpu.make_async_remote_copy(
            src_ref=state.at[half_rows(h), :],
            dst_ref=other.at[half_rows(h), :],
            send_sem=swap_sem.at[0, h],
            recv_sem=swap_sem.at[1, h],
            device_id=dev(mate, t),
            device_id_type=MESH,
        )

    def tot_copy(h, target, source):
        return pltpu.make_async_remote_copy(
            src_ref=total.at[half_rows(h), :],
            dst_ref=totals.at[source, half_rows(h), :],
            send_sem=tot_send.at[h, target],
            recv_sem=tot_recv.at[h, source],
            device_id=dev(2 * target + c, t),
            device_id_type=MESH,
        )

    def send_totals(h):
        rows = half_rows(h)
        swap(h).wait_recv()

        @pl.when(c == 0)
        def _():
            total[rows, :] = (decay_sec[rows, :] * state[rows, :] + other[rows, :]).astype(
                total.dtype
            )

        @pl.when(c == 1)
        def _():
            total[rows, :] = (decay_sec[rows, :] * other[rows, :] + state[rows, :]).astype(
                total.dtype
            )

        for k in range(1, nz):

            @pl.when(k > z)
            def _(k=k):
                tot_copy(h, k, z).start()

    def entering(h):
        rows = half_rows(h)
        enter[rows, :] = jnp.zeros((span, LANES), jnp.float32)
        for k in range(nz - 1):

            @pl.when(k < z)
            def _(k=k):
                tot_copy(h, z, k).wait_recv()
                both = decay_sec[rows, :] * decay_sec[rows, :]
                enter[rows, :] = enter[rows, :] * both + totals[k, rows, :].astype(jnp.float32)

        @pl.when(c == 1)
        def _():
            enter[rows, :] = decay_sec[rows, :] * enter[rows, :] + other[rows, :]

    def fix(h):
        def step(i, carried):
            rows = pl.ds(pl.multiple_of(i * groups + h * width, width), width)
            prod[rows, :] = prod[rows, :] + tree(list(carried))
            return tuple(u * mode_rows(decay, m, h) for m, u in enumerate(carried))

        lax.fori_loop(
            0,
            tok,
            step,
            tuple(
                mode_rows(gain, m, h) * mode_rows(decay, m, h) * mode_rows(enter, m, h)
                for m in range(modes)
            ),
            unroll=4,
        )
        for g in range(h * width, (h + 1) * width):
            lanes = pl.ds(g * LANES, LANES)
            mixed[:, lanes] = (qf[:, lanes] * prod[pl.ds(g, tok, stride=groups), :]).astype(
                mixed.dtype
            )

    def share(p, index):
        return pl.ds(pl.multiple_of(p * rows_part + index * piece, piece), piece)

    def half_lanes(h):
        return pl.ds(h * width * LANES, width * LANES)

    def s1_copy(h, p, target, source):
        return pltpu.make_async_remote_copy(
            src_ref=mixed.at[share(p, target), half_lanes(h)],
            dst_ref=stage.at[p, source, :, half_lanes(h)],
            send_sem=s1_send.at[h, p, target],
            recv_sem=s1_recv.at[h, p, source],
            device_id=dev(s, target),
            device_id_type=MESH,
        )

    def s1_local(h, p):
        return pltpu.make_async_copy(
            mixed.at[share(p, t), half_lanes(h)],
            stage.at[p, t, :, half_lanes(h)],
            s1_recv.at[h, p, t],
        )

    def each_peer(body):
        def one(d, carry):
            body((t + d) % nt)
            return carry

        lax.fori_loop(1, nt, one, 0)

    def scatter(h):
        for p in range(parts):
            each_peer(lambda q: s1_copy(h, p, q, t).start())
            s1_local(h, p).start()

    def scattered(h, p, k):
        @pl.when(k == t)
        def _():
            s1_local(h, p).wait()

        @pl.when(k != t)
        def _():
            s1_copy(h, p, t, k).wait_recv()

    def s2_copy(h, p, target, source):
        return pltpu.make_async_remote_copy(
            src_ref=stage.at[p, target, :, half_lanes(h)],
            dst_ref=full.at[source, share(p, t), half_lanes(h)],
            send_sem=s2_send.at[h, p, target],
            recv_sem=s2_recv.at[h, p, source],
            device_id=dev(2 * target + c, t),
            device_id_type=MESH,
        )

    def s2_local(h, p):
        return pltpu.make_async_copy(
            stage.at[p, z, :, half_lanes(h)],
            full.at[z, share(p, t), half_lanes(h)],
            s2_recv.at[h, p, z],
        )

    candidates = 2 * (nz - 1) * parts

    def each_plane(f, body):
        p = (f // 2) % parts
        d = nz - 1 - f // (2 * parts)
        k = z + d * (1 - 2 * (f % 2))

        @pl.when((k >= 0) & (k < nz))
        def _():
            body(k, p)

    def loop_planes(body):
        def one(f, carry):
            each_plane(f, body)
            return carry

        lax.fori_loop(0, candidates, one, 0)

    def to_planes(h):
        def go(k, p):
            scattered(h, p, k)
            s2_copy(h, p, k, z).start()

        loop_planes(go)
        for p in range(parts):
            scattered(h, p, z)
            s2_local(h, p).start()

    for g in range(groups):
        lanes = pl.ds(g * LANES, LANES)
        rows = pl.ds((g // width) * span + g % width, modes, stride=width)
        r = rate[:, lanes]
        decay[rows, :] = jnp.exp(-r)
        decay_sec[rows, :] = jnp.exp(-r * tok)
        gain[rows, :] = residue[:, lanes] * jnp.sqrt(one_minus_exp(2.0 * r))
        skip[g : g + 1, :] = skip_row[:, lanes]

    keys_values(0)
    pl.semaphore_wait(barrier, ns - 1 + nt - 1)

    @pl.when(s < ns - 1)
    def _():
        halo_copy.start()

    @pl.when(s == 0)
    def _():
        halo[...] = jnp.zeros_like(halo)

    @pl.when(s > 0)
    def _():
        halo_copy.wait_recv()

    first_rows(0)
    for h in range(halves):
        if h > 0:
            keys_values(h)
            first_rows(h)
            send_totals(h - 1)
        recur(h)
        swap(h).start()
    queries(0)
    send_totals(halves - 1)
    w_remote.start()
    w_local.start()
    for h in range(halves):
        if h > 0:
            queries(h)
        entering(h)
        fix(h)
        scatter(h)
    for h in range(halves):
        to_planes(h)

    def s3_copy(target, source, k, p):
        rows = full.at[k, share(p, source), :]
        return pltpu.make_async_remote_copy(
            src_ref=rows,
            dst_ref=rows,
            send_sem=s3_send.at[k * parts + p, target],
            recv_sem=s3_recv.at[k * parts + p, source],
            device_id=dev(s, target),
            device_id_type=MESH,
        )

    def spread(k, p):
        each_peer(lambda q: s3_copy(q, t, k, p).start())

    def spread_received(k, p):
        for h in range(halves):
            s2_copy(h, p, z, k).wait_recv()
        spread(k, p)

    def gathered(k, p):
        each_peer(lambda q: s3_copy(t, q, k, p).wait_recv())

    tile = min(512, cols)

    def part_rows(p):
        return pl.ds(pl.multiple_of(p * rows_part, rows_part), rows_part)

    def product(k, p, store):
        def one(n, carry):
            lanes = pl.ds(pl.multiple_of(n * tile, tile), tile)
            store(
                lanes,
                jnp.dot(
                    full[k, part_rows(p), :],
                    wfull[:, lanes],
                    preferred_element_type=jnp.float32,
                ),
            )
            return carry

        lax.fori_loop(0, cols // tile, one, 0)

    def rs_copy(k, p, slot, target):
        return pltpu.make_async_remote_copy(
            src_ref=part.at[k, part_rows(p), :],
            dst_ref=recv.at[slot, part_rows(p), :],
            send_sem=rs_send.at[k, p],
            recv_sem=rs_recv.at[slot, p],
            device_id=dev(2 * target + c, t),
            device_id_type=MESH,
        )

    def rs_wait(slot, p):
        rs_copy(z, p, slot, z).wait_recv()

    def contribute(k, p):
        gathered(k, p)
        rows = part_rows(p)

        def fresh(lanes, value):
            part[k, rows, lanes] = value.astype(part.dtype)

        def added(lanes, value):
            part[k, rows, lanes] = (value + recv[k, rows, lanes].astype(jnp.float32)).astype(
                part.dtype
            )

        first = ((k > z) & (z == 0)) | ((k < z) & (z == nz - 1))

        @pl.when(first)
        def _():
            product(k, p, fresh)

        @pl.when(jnp.logical_not(first))
        def _():
            rs_wait(k, p)
            product(k, p, added)

        @pl.when(k > z)
        def _():
            rs_copy(k, p, k, z + 1).start()

        @pl.when(k < z - 1)
        def _():
            rs_copy(k, p, k, z - 1).start()

        @pl.when(k == z - 1)
        def _():
            rs_copy(k, p, nz, z - 1).start()

    lead = 2
    for f in range(lead):
        each_plane(f, spread_received)
    for p in range(parts):
        for h in range(halves):
            s2_local(h, p).wait()
        spread(z, p)
    w_local.wait()
    w_remote.wait_recv()

    def one_plane(f, carry):
        @pl.when(f + lead < candidates)
        def _():
            each_plane(f + lead, spread_received)

        each_plane(f, contribute)
        return carry

    lax.fori_loop(0, candidates, one_plane, 0)

    for p in range(parts):
        gathered(z, p)

        def keep_own(lanes, value, p=p):
            own[part_rows(p), lanes] = value

        product(z, p, keep_own)

    for p in range(parts):
        rows = part_rows(p)

        @pl.when(z > 0)
        def _(p=p, rows=rows):
            rs_wait(z, p)
            own[rows, :] += recv[z, rows, :].astype(jnp.float32)

        @pl.when(z < nz - 1)
        def _(p=p, rows=rows):
            rs_wait(nz, p)
            own[rows, :] += recv[nz, rows, :].astype(jnp.float32)

        out[rows, :] = own[rows, :].astype(out.dtype)

    @pl.when(s < ns - 1)
    def _():
        halo_copy.wait_send()

    w_remote.wait_send()
    for h in range(halves):
        swap(h).wait_send()
        for k in range(1, nz):

            @pl.when(k > z)
            def _(k=k, h=h):
                tot_copy(h, k, z).wait_send()

        for p in range(parts):
            each_peer(lambda q, h=h, p=p: s1_copy(h, p, q, t).wait_send())
        loop_planes(lambda k, p, h=h: s2_copy(h, p, k, z).wait_send())

    def all_sent(k, p):
        each_peer(lambda q: s3_copy(q, t, k, p).wait_send())

    for p in range(parts):
        all_sent(z, p)
    loop_planes(all_sent)
    loop_planes(lambda k, p: rs_copy(k, p, k, z).wait_send())


def local(ns, nt, qkv, conv_weight, decay_rate, residue, skip_gain, out_weight):
    tok, ch = qkv.shape[1], qkv.shape[2]
    modes = decay_rate.shape[0]
    groups = ch // LANES
    nz = ns // 2
    cols = out_weight.shape[1]
    rows = modes * groups
    parts = token_parts(tok, nt)
    halves = groups // min(8, groups)
    vmem = pl.BlockSpec(memory_space=pltpu.VMEM)
    f32, bf16 = jnp.float32, jnp.bfloat16
    dma = pltpu.SemaphoreType.DMA
    return pl.pallas_call(
        functools.partial(kernel, ns, nt, modes),
        out_shape=jax.ShapeDtypeStruct((tok, cols), bf16),
        in_specs=[vmem] * 5 + [pl.BlockSpec(memory_space=pl.ANY)],
        out_specs=vmem,
        scratch_shapes=[
            pltpu.VMEM((rows, LANES), f32),
            pltpu.VMEM((rows, LANES), f32),
            pltpu.VMEM((rows, LANES), f32),
            pltpu.VMEM((groups, LANES), f32),
            pltpu.VMEM((3, HALO, ch), bf16),
            pltpu.VMEM((3, HALO + tok, LANES), f32),
            pltpu.VMEM((tok * groups, LANES), f32),
            pltpu.VMEM((tok, ch), f32),
            pltpu.VMEM((tok, ch), bf16),
            pltpu.VMEM((ch, cols), bf16),
            pltpu.VMEM((rows, LANES), f32),
            pltpu.VMEM((rows, LANES), f32),
            pltpu.VMEM((rows, LANES), bf16),
            pltpu.VMEM((nz, rows, LANES), bf16),
            pltpu.VMEM((rows, LANES), f32),
            pltpu.VMEM((parts, nt, tok // parts // nt, ch), bf16),
            pltpu.VMEM((nz, tok, ch), bf16),
            pltpu.VMEM((nz, tok, cols), bf16),
            pltpu.VMEM((nz + 1, tok, cols), bf16),
            pltpu.VMEM((tok, cols), f32),
            dma((2,)),
            dma((3,)),
            dma((2, halves)),
            dma((halves, nz)),
            dma((halves, nz)),
            dma((halves, parts, nt)),
            dma((halves, parts, nt)),
            dma((halves, parts, nz)),
            dma((halves, parts, nz)),
            dma((nz * parts, nt)),
            dma((nz * parts, nt)),
            dma((nz, parts)),
            dma((nz + 1, parts)),
        ],
        compiler_params=pltpu.CompilerParams(
            collective_id=0, has_side_effects=True, vmem_limit_bytes=56 * 1024 * 1024
        ),
        cost_estimate=pl.CostEstimate(
            flops=2 * tok * nz * ch * cols, bytes_accessed=12 * 1024 * 1024, transcendentals=0
        ),
    )(
        qkv,
        conv_weight,
        decay_rate,
        residue,
        skip_gain.reshape(1, ch),
        out_weight,
    )


def solution(mesh):
    return jax.shard_map(
        functools.partial(local, mesh.shape["seq"], mesh.shape["tensor"]),
        mesh=mesh,
        in_specs=(
            P(None, "seq", "tensor"),
            P(None, None, "tensor"),
            P(None, "tensor"),
            P(None, "tensor"),
            P("tensor"),
            P("seq", "tensor"),
        ),
        out_specs=P("seq", "tensor"),
        check_vma=False,
    )
```

```python
import functools

import jax
import jax.numpy as jnp
from jax import lax
from jax.experimental import pallas as pl
from jax.experimental.pallas import tpu as pltpu
from jax.sharding import PartitionSpec as P

MESH = pl.DeviceIdType.MESH
LANES = 128
HALO = 16


def token_parts(tok, nt):
    return next(n for n in (4, 2, 1) if tok % (n * nt * HALO) == 0)


def one_minus_exp(x):
    small = jnp.ones_like(x)
    for n in range(9, 1, -1):
        small = 1.0 - small * x * (1.0 / n)
    return jnp.where(x < 0.25, x * small, 1.0 - jnp.exp(-x))


def kernel(
    ns,
    nt,
    modes,
    qkv,
    conv_w,
    rate,
    residue,
    skip_row,
    weight,
    out,
    decay,
    decay_sec,
    gain,
    skip,
    halo,
    ext,
    prod,
    qf,
    mixed,
    wfull,
    state,
    other,
    total,
    totals,
    enter,
    stage,
    full,
    part,
    recv,
    own,
    halo_sem,
    w_sem,
    swap_sem,
    tot_send,
    tot_recv,
    s1_send,
    s1_recv,
    s2_send,
    s2_recv,
    s3_send,
    s3_recv,
    rs_send,
    rs_recv,
):
    nz = ns // 2
    tok = qkv.shape[1]
    ch = qkv.shape[2]
    groups = ch // LANES
    parts = token_parts(tok, nt)
    rows_part = tok // parts
    piece = rows_part // nt
    width = min(8, groups)
    halves = groups // width
    span = modes * width
    rows_w = weight.shape[0]
    cols = weight.shape[1]
    s = lax.axis_index("seq")
    t = lax.axis_index("tensor")
    z = s // 2
    c = s % 2
    mate = 2 * z + (1 - c)

    def dev(seq, ten):
        return (seq, ten)

    barrier = pltpu.get_barrier_semaphore()
    for d in range(1, ns):
        pl.semaphore_signal(barrier, inc=1, device_id=dev((s + d) % ns, t), device_id_type=MESH)
    for d in range(1, nt):
        pl.semaphore_signal(barrier, inc=1, device_id=dev(s, (t + d) % nt), device_id_type=MESH)

    halo_copy = pltpu.make_async_remote_copy(
        src_ref=qkv.at[:, pl.ds(tok - HALO, HALO), :],
        dst_ref=halo,
        send_sem=halo_sem.at[0],
        recv_sem=halo_sem.at[1],
        device_id=dev((s + 1) % ns, t),
        device_id_type=MESH,
    )

    w_rows = pl.ds(pl.multiple_of(c * rows_w, rows_w), rows_w)
    w_remote = pltpu.make_async_remote_copy(
        src_ref=weight,
        dst_ref=wfull.at[w_rows, :],
        send_sem=w_sem.at[0],
        recv_sem=w_sem.at[1],
        device_id=dev(mate, t),
        device_id_type=MESH,
    )
    w_local = pltpu.make_async_copy(weight, wfull.at[w_rows, :], w_sem.at[2])

    def short(i, lanes, head, count):
        ext[i, 0:HALO, :] = head
        ext[i, HALO : HALO + count, :] = qkv[i, 0:count, lanes].astype(jnp.float32)
        taps = conv_w[i, :, lanes]
        return (
            taps[0:1] * ext[i, HALO : HALO + count, :]
            + taps[1:2] * ext[i, HALO - 1 : HALO - 1 + count, :]
            + taps[2:3] * ext[i, HALO - 2 : HALO - 2 + count, :]
        )

    def before(i, lanes):
        return halo[i, :, lanes].astype(jnp.float32)

    def mode_rows(ref, m, h):
        return ref[h * span + m * width : h * span + (m + 1) * width, :]

    def half_rows(h):
        return pl.ds(h * span, span)

    def tree(values):
        while len(values) > 1:
            values = [a + b for a, b in zip(values[::2], values[1::2])] + (
                [values[-1]] if len(values) % 2 else []
            )
        return values[0]

    def keys_values(h):
        zero = jnp.zeros((HALO, LANES), jnp.float32)
        for g in range(h * width, (h + 1) * width):
            lanes = pl.ds(g * LANES, LANES)
            prod[pl.ds(g, tok, stride=groups), :] = short(1, lanes, zero, tok) * short(
                2, lanes, zero, tok
            )

    def first_rows(h):
        for g in range(h * width, (h + 1) * width):
            lanes = pl.ds(g * LANES, LANES)
            prod[pl.ds(g, HALO, stride=groups), :] = short(
                1, lanes, before(1, lanes), HALO
            ) * short(2, lanes, before(2, lanes), HALO)

    def queries(h):
        for g in range(h * width, (h + 1) * width):
            lanes = pl.ds(g * LANES, LANES)
            qf[:, lanes] = short(0, lanes, before(0, lanes), tok)

    def recur(h):
        skips = skip[h * width : (h + 1) * width, :]

        def step(i, states):
            rows = pl.ds(pl.multiple_of(i * groups + h * width, width), width)
            x = prod[rows, :]
            new = tuple(st * mode_rows(decay, m, h) + x for m, st in enumerate(states))
            terms = [st * mode_rows(gain, m, h) for m, st in enumerate(new)]
            prod[rows, :] = tree(terms) + skips * x
            return new

        states = lax.fori_loop(
            0,
            tok,
            step,
            tuple(jnp.zeros((width, LANES), jnp.float32) for _ in range(modes)),
            unroll=4,
        )
        for m in range(modes):
            state[h * span + m * width : h * span + (m + 1) * width, :] = states[m]

    def swap(h):
        return pltpu.make_async_remote_copy(
            src_ref=state.at[half_rows(h), :],
            dst_ref=other.at[half_rows(h), :],
            send_sem=swap_sem.at[0, h],
            recv_sem=swap_sem.at[1, h],
            device_id=dev(mate, t),
            device_id_type=MESH,
        )

    def tot_copy(h, target, source):
        return pltpu.make_async_remote_copy(
            src_ref=total.at[half_rows(h), :],
            dst_ref=totals.at[source, half_rows(h), :],
            send_sem=tot_send.at[h, target],
            recv_sem=tot_recv.at[h, source],
            device_id=dev(2 * target + c, t),
            device_id_type=MESH,
        )

    def send_totals(h):
        rows = half_rows(h)
        swap(h).wait_recv()

        @pl.when(c == 0)
        def _():
            total[rows, :] = (decay_sec[rows, :] * state[rows, :] + other[rows, :]).astype(
                total.dtype
            )

        @pl.when(c == 1)
        def _():
            total[rows, :] = (decay_sec[rows, :] * other[rows, :] + state[rows, :]).astype(
                total.dtype
            )

        for k in range(1, nz):

            @pl.when(k > z)
            def _(k=k):
                tot_copy(h, k, z).start()

    def entering(h):
        rows = half_rows(h)
        enter[rows, :] = jnp.zeros((span, LANES), jnp.float32)
        for k in range(nz - 1):

            @pl.when(k < z)
            def _(k=k):
                tot_copy(h, z, k).wait_recv()
                both = decay_sec[rows, :] * decay_sec[rows, :]
                enter[rows, :] = enter[rows, :] * both + totals[k, rows, :].astype(jnp.float32)

        @pl.when(c == 1)
        def _():
            enter[rows, :] = decay_sec[rows, :] * enter[rows, :] + other[rows, :]

    def fix(h):
        def step(i, carried):
            rows = pl.ds(pl.multiple_of(i * groups + h * width, width), width)
            prod[rows, :] = prod[rows, :] + tree(list(carried))
            return tuple(u * mode_rows(decay, m, h) for m, u in enumerate(carried))

        lax.fori_loop(
            0,
            tok,
            step,
            tuple(
                mode_rows(gain, m, h) * mode_rows(decay, m, h) * mode_rows(enter, m, h)
                for m in range(modes)
            ),
            unroll=4,
        )
        for g in range(h * width, (h + 1) * width):
            lanes = pl.ds(g * LANES, LANES)
            mixed[:, lanes] = (qf[:, lanes] * prod[pl.ds(g, tok, stride=groups), :]).astype(
                mixed.dtype
            )

    def share(p, index):
        return pl.ds(pl.multiple_of(p * rows_part + index * piece, piece), piece)

    def half_lanes(h):
        return pl.ds(h * width * LANES, width * LANES)

    def s1_copy(h, p, target, source):
        return pltpu.make_async_remote_copy(
            src_ref=mixed.at[share(p, target), half_lanes(h)],
            dst_ref=stage.at[p, source, :, half_lanes(h)],
            send_sem=s1_send.at[h, p, target],
            recv_sem=s1_recv.at[h, p, source],
            device_id=dev(s, target),
            device_id_type=MESH,
        )

    def s1_local(h, p):
        return pltpu.make_async_copy(
            mixed.at[share(p, t), half_lanes(h)],
            stage.at[p, t, :, half_lanes(h)],
            s1_recv.at[h, p, t],
        )

    def each_peer(body):
        def one(d, carry):
            body((t + d) % nt)
            return carry

        lax.fori_loop(1, nt, one, 0)

    def scatter(h):
        for p in range(parts):
            each_peer(lambda q: s1_copy(h, p, q, t).start())
            s1_local(h, p).start()

    def scattered(h, p, k):
        @pl.when(k == t)
        def _():
            s1_local(h, p).wait()

        @pl.when(k != t)
        def _():
            s1_copy(h, p, t, k).wait_recv()

    def s2_copy(h, p, target, source):
        return pltpu.make_async_remote_copy(
            src_ref=stage.at[p, target, :, half_lanes(h)],
            dst_ref=full.at[source, share(p, t), half_lanes(h)],
            send_sem=s2_send.at[h, p, target],
            recv_sem=s2_recv.at[h, p, source],
            device_id=dev(2 * target + c, t),
            device_id_type=MESH,
        )

    def s2_local(h, p):
        return pltpu.make_async_copy(
            stage.at[p, z, :, half_lanes(h)],
            full.at[z, share(p, t), half_lanes(h)],
            s2_recv.at[h, p, z],
        )

    candidates = 2 * (nz - 1) * parts

    def each_plane(f, body):
        p = (f // 2) % parts
        d = nz - 1 - f // (2 * parts)
        k = z + d * (1 - 2 * (f % 2))

        @pl.when((k >= 0) & (k < nz))
        def _():
            body(k, p)

    def loop_planes(body):
        def one(f, carry):
            each_plane(f, body)
            return carry

        lax.fori_loop(0, candidates, one, 0)

    def to_planes(h):
        def go(k, p):
            scattered(h, p, k)
            s2_copy(h, p, k, z).start()

        loop_planes(go)
        for p in range(parts):
            scattered(h, p, z)
            s2_local(h, p).start()

    for g in range(groups):
        lanes = pl.ds(g * LANES, LANES)
        rows = pl.ds((g // width) * span + g % width, modes, stride=width)
        r = rate[:, lanes]
        decay[rows, :] = jnp.exp(-r)
        decay_sec[rows, :] = jnp.exp(-r * tok)
        gain[rows, :] = residue[:, lanes] * jnp.sqrt(one_minus_exp(2.0 * r))
        skip[g : g + 1, :] = skip_row[:, lanes]

    keys_values(0)
    pl.semaphore_wait(barrier, ns - 1 + nt - 1)

    @pl.when(s < ns - 1)
    def _():
        halo_copy.start()

    @pl.when(s == 0)
    def _():
        halo[...] = jnp.zeros_like(halo)

    @pl.when(s > 0)
    def _():
        halo_copy.wait_recv()

    first_rows(0)
    for h in range(halves):
        if h > 0:
            keys_values(h)
            first_rows(h)
            send_totals(h - 1)
        recur(h)
        swap(h).start()
    queries(0)
    send_totals(halves - 1)
    w_remote.start()
    w_local.start()
    for h in range(halves):
        if h > 0:
            queries(h)
        entering(h)
        fix(h)
        scatter(h)
    for h in range(halves):
        to_planes(h)

    def s3_copy(target, source, k, p):
        rows = full.at[k, share(p, source), :]
        return pltpu.make_async_remote_copy(
            src_ref=rows,
            dst_ref=rows,
            send_sem=s3_send.at[k * parts + p, target],
            recv_sem=s3_recv.at[k * parts + p, source],
            device_id=dev(s, target),
            device_id_type=MESH,
        )

    def spread(k, p):
        each_peer(lambda q: s3_copy(q, t, k, p).start())

    def spread_received(k, p):
        for h in range(halves):
            s2_copy(h, p, z, k).wait_recv()
        spread(k, p)

    def gathered(k, p):
        each_peer(lambda q: s3_copy(t, q, k, p).wait_recv())

    tile = min(512, cols)

    def part_rows(p):
        return pl.ds(pl.multiple_of(p * rows_part, rows_part), rows_part)

    def product(k, p, store):
        def one(n, carry):
            lanes = pl.ds(pl.multiple_of(n * tile, tile), tile)
            store(
                lanes,
                jnp.dot(
                    full[k, part_rows(p), :],
                    wfull[:, lanes],
                    preferred_element_type=jnp.float32,
                ),
            )
            return carry

        lax.fori_loop(0, cols // tile, one, 0)

    def rs_copy(k, p, slot, target):
        return pltpu.make_async_remote_copy(
            src_ref=part.at[k, part_rows(p), :],
            dst_ref=recv.at[slot, part_rows(p), :],
            send_sem=rs_send.at[k, p],
            recv_sem=rs_recv.at[slot, p],
            device_id=dev(2 * target + c, t),
            device_id_type=MESH,
        )

    def rs_wait(slot, p):
        rs_copy(z, p, slot, z).wait_recv()

    def contribute(k, p):
        gathered(k, p)
        rows = part_rows(p)

        def hold(lanes, value):
            own[rows, lanes] = value

        product(k, p, hold)
        first = ((k > z) & (z == 0)) | ((k < z) & (z == nz - 1))

        @pl.when(first)
        def _():
            part[k, rows, :] = own[rows, :].astype(part.dtype)

        @pl.when(jnp.logical_not(first))
        def _():
            rs_wait(k, p)
            part[k, rows, :] = (own[rows, :] + recv[k, rows, :].astype(jnp.float32)).astype(
                part.dtype
            )

        @pl.when(k > z)
        def _():
            rs_copy(k, p, k, z + 1).start()

        @pl.when(k < z - 1)
        def _():
            rs_copy(k, p, k, z - 1).start()

        @pl.when(k == z - 1)
        def _():
            rs_copy(k, p, nz, z - 1).start()

    lead = 2
    for f in range(lead):
        each_plane(f, spread_received)
    for p in range(parts):
        for h in range(halves):
            s2_local(h, p).wait()
        spread(z, p)
    w_local.wait()
    w_remote.wait_recv()

    def one_plane(f, carry):
        @pl.when(f + lead < candidates)
        def _():
            each_plane(f + lead, spread_received)

        each_plane(f, contribute)
        return carry

    lax.fori_loop(0, candidates, one_plane, 0)

    for p in range(parts):
        gathered(z, p)

        def keep_own(lanes, value, p=p):
            own[part_rows(p), lanes] = value

        product(z, p, keep_own)

    for p in range(parts):
        rows = part_rows(p)

        @pl.when(z > 0)
        def _(p=p, rows=rows):
            rs_wait(z, p)
            own[rows, :] += recv[z, rows, :].astype(jnp.float32)

        @pl.when(z < nz - 1)
        def _(p=p, rows=rows):
            rs_wait(nz, p)
            own[rows, :] += recv[nz, rows, :].astype(jnp.float32)

        out[rows, :] = own[rows, :].astype(out.dtype)

    @pl.when(s < ns - 1)
    def _():
        halo_copy.wait_send()

    w_remote.wait_send()
    for h in range(halves):
        swap(h).wait_send()
        for k in range(1, nz):

            @pl.when(k > z)
            def _(k=k, h=h):
                tot_copy(h, k, z).wait_send()

        for p in range(parts):
            each_peer(lambda q, h=h, p=p: s1_copy(h, p, q, t).wait_send())
        loop_planes(lambda k, p, h=h: s2_copy(h, p, k, z).wait_send())

    def all_sent(k, p):
        each_peer(lambda q: s3_copy(q, t, k, p).wait_send())

    for p in range(parts):
        all_sent(z, p)
    loop_planes(all_sent)
    loop_planes(lambda k, p: rs_copy(k, p, k, z).wait_send())


def local(ns, nt, qkv, conv_weight, decay_rate, residue, skip_gain, out_weight):
    tok, ch = qkv.shape[1], qkv.shape[2]
    modes = decay_rate.shape[0]
    groups = ch // LANES
    nz = ns // 2
    cols = out_weight.shape[1]
    rows = modes * groups
    parts = token_parts(tok, nt)
    halves = groups // min(8, groups)
    vmem = pl.BlockSpec(memory_space=pltpu.VMEM)
    f32, bf16 = jnp.float32, jnp.bfloat16
    dma = pltpu.SemaphoreType.DMA
    return pl.pallas_call(
        functools.partial(kernel, ns, nt, modes),
        out_shape=jax.ShapeDtypeStruct((tok, cols), bf16),
        in_specs=[vmem] * 5 + [pl.BlockSpec(memory_space=pl.ANY)],
        out_specs=vmem,
        scratch_shapes=[
            pltpu.VMEM((rows, LANES), f32),
            pltpu.VMEM((rows, LANES), f32),
            pltpu.VMEM((rows, LANES), f32),
            pltpu.VMEM((groups, LANES), f32),
            pltpu.VMEM((3, HALO, ch), bf16),
            pltpu.VMEM((3, HALO + tok, LANES), f32),
            pltpu.VMEM((tok * groups, LANES), f32),
            pltpu.VMEM((tok, ch), f32),
            pltpu.VMEM((tok, ch), bf16),
            pltpu.VMEM((ch, cols), bf16),
            pltpu.VMEM((rows, LANES), f32),
            pltpu.VMEM((rows, LANES), f32),
            pltpu.VMEM((rows, LANES), bf16),
            pltpu.VMEM((nz, rows, LANES), bf16),
            pltpu.VMEM((rows, LANES), f32),
            pltpu.VMEM((parts, nt, tok // parts // nt, ch), bf16),
            pltpu.VMEM((nz, tok, ch), bf16),
            pltpu.VMEM((nz, tok, cols), bf16),
            pltpu.VMEM((nz + 1, tok, cols), bf16),
            pltpu.VMEM((tok, cols), f32),
            dma((2,)),
            dma((3,)),
            dma((2, halves)),
            dma((halves, nz)),
            dma((halves, nz)),
            dma((halves, parts, nt)),
            dma((halves, parts, nt)),
            dma((halves, parts, nz)),
            dma((halves, parts, nz)),
            dma((nz * parts, nt)),
            dma((nz * parts, nt)),
            dma((nz, parts)),
            dma((nz + 1, parts)),
        ],
        compiler_params=pltpu.CompilerParams(
            collective_id=0, has_side_effects=True, vmem_limit_bytes=56 * 1024 * 1024
        ),
        cost_estimate=pl.CostEstimate(
            flops=2 * tok * nz * ch * cols, bytes_accessed=12 * 1024 * 1024, transcendentals=0
        ),
    )(
        qkv,
        conv_weight,
        decay_rate,
        residue,
        skip_gain.reshape(1, ch),
        out_weight,
    )


def solution(mesh):
    return jax.shard_map(
        functools.partial(local, mesh.shape["seq"], mesh.shape["tensor"]),
        mesh=mesh,
        in_specs=(
            P(None, "seq", "tensor"),
            P(None, None, "tensor"),
            P(None, "tensor"),
            P(None, "tensor"),
            P("tensor"),
            P("seq", "tensor"),
        ),
        out_specs=P("seq", "tensor"),
        check_vma=False,
    )
```
